32 devices in a mesh: dp: 4 (over y, x), tensor: 8 (over z, core).
Axes of the slice: x: 2, y: 2, z: 4, core: 2. Of those that a mesh axis runs over, the one named last changes fastest.
Arguments:
- tokens: float32 [1376, 8, 1024], P('tensor', 'dp'), may hold values from -6 to 6
- cotangent: float32 [1376, 8, 1024], P('tensor', 'dp'), may hold values from -6 to 6
- attention_in: float32 [2, 1024, 3072], P(None, 'dp', 'tensor'), may hold values from -0.1875 to 0.1875
- attention_out: float32 [2, 1024, 1024], P(None, 'dp', 'tensor'), may hold values from -0.75 to 0.75
- hidden_up: float32 [2, 1024, 4096], P(None, 'dp', 'tensor'), may hold values from -0.1875 to 0.1875
- hidden_down: float32 [2, 1024, 4096], P(None, 'dp', 'tensor'), may hold values from -0.09375 to 0.09375
- attention_in_momentum: float32 [2, 1024, 3072], P(None, 'dp', 'tensor')
- attention_out_momentum: float32 [2, 1024, 1024], P(None, 'dp', 'tensor')
- hidden_up_momentum: float32 [2, 1024, 4096], P(None, 'dp', 'tensor')
- hidden_down_momentum: float32 [2, 1024, 4096], P(None, 'dp', 'tensor')
- row_params: float32 [2, 8, 1024], replicated, may hold values from -1.2 to 1.5
- column_bias: float32 [2, 16, 384], P(None, 'tensor'), may hold values from -1.5 to 1.5
- lengths: int32 [8], P('dp'), may hold values from 344 to 1376, as said below
Outputs:
- layer_output: float32 [1376, 8, 1024], P('tensor', 'dp')
- tokens_grad: float32 [1376, 8, 1024], P('tensor', 'dp')
- attention_in_grad: float32 [2, 1024, 3072], P(None, 'dp', 'tensor')
- attention_out_grad: float32 [2, 1024, 1024], P(None, 'dp', 'tensor')
- hidden_up_grad: float32 [2, 1024, 4096], P(None, 'dp', 'tensor')
- hidden_down_grad: float32 [2, 1024, 4096], P(None, 'dp', 'tensor')
- attention_in_momentum_new: float32 [2, 1024, 3072], P(None, 'dp', 'tensor')
- attention_out_momentum_new: float32 [2, 1024, 1024], P(None, 'dp', 'tensor')
- hidden_up_momentum_new: float32 [2, 1024, 4096], P(None, 'dp', 'tensor')
- hidden_down_momentum_new: float32 [2, 1024, 4096], P(None, 'dp', 'tensor')
- attention_in_new: float32 [2, 1024, 3072], P(None, 'dp', 'tensor')
- attention_out_new: float32 [2, 1024, 1024], P(None, 'dp', 'tensor')
- hidden_up_new: float32 [2, 1024, 4096], P(None, 'dp', 'tensor')
- hidden_down_new: float32 [2, 1024, 4096], P(None, 'dp', 'tensor')
- row_grad: float32 [2, 8, 1024], replicated
- row_new: float32 [2, 8, 1024], replicated
- column_grad: float32 [2, 16, 384], P(None, 'tensor', 'dp')
- column_new: float32 [2, 16, 384], P(None, 'tensor', 'dp')
The draws below stay inside these ranges and needn't reach their ends.
Inputs may be any that keep to these rules, and one draw needn't show every extreme that they name: `lengths`: in each block of 2 images of one index of dp, one image, drawn from the seed, has exactly 1376 valid positions.
All inputs are finite; a program needn't handle non-finite values.
Results may differ from the reference program's by a relative error of at most 0.012.
Values may be sent and summed in bfloat16 or wider, within the bound.
No kernel may reach another device: no remote copies, remote signals or barrier semaphores. Data moves between devices by JAX's collectives and lax.ppermute only.
A program may use at most 320 MiB of HBM per device.

```python
import math
import jax
import jax.numpy as jnp
from jax import lax

D = 1024
HEADS = 16
HD = 64
FF = 4096
SEQ = 1376
LAYERS = 2
NS_STEPS = 5
IMG_DP = 2
IMAGES = 8
N_DP = 4


def momentum_field(key, columns, spread):
    key_noise, key_size, key_sign = jax.random.split(key, 3)
    noise = spread * jax.random.normal(key_noise, (LAYERS, D, columns), jnp.float32)
    row_ids = jnp.arange(D)[:, None]
    col_ids = jnp.arange(columns)[None, :]
    on_diagonal = col_ids % D == row_ids
    magnitude = jax.random.uniform(key_size, (LAYERS, D, columns), jnp.float32, 1.0, 2.0)
    signs = jnp.where(jax.random.bernoulli(key_sign, 0.5, (LAYERS, D, columns)), 1.0, -1.0)
    diagonal = 8.0 * spread * D ** 0.5 * magnitude * signs
    return noise + jnp.where(on_diagonal[None], diagonal, 0.0)


def draw_attention_in_momentum(key, part):
    key = jax.random.fold_in(key, 21)
    return momentum_field(key, 3 * D, 0.3 * (IMAGES * SEQ) ** 0.5)


def draw_attention_out_momentum(key, part):
    key = jax.random.fold_in(key, 22)
    return momentum_field(key, D, 0.2 * (IMAGES * SEQ) ** 0.5)


def draw_hidden_up_momentum(key, part):
    key = jax.random.fold_in(key, 23)
    return momentum_field(key, FF, 0.25 * (IMAGES * SEQ) ** 0.5)


def draw_hidden_down_momentum(key, part):
    key = jax.random.fold_in(key, 24)
    return momentum_field(key, FF, 0.5 * (IMAGES * SEQ) ** 0.5)


def draw_row_params(key, part):
    key = jax.random.fold_in(key, 7)
    key_gain, key_shift, key_scale = jax.random.split(key, 3)
    gains = jax.random.uniform(key_gain, (LAYERS, 8, D), jnp.float32, 0.6, 1.4)
    shifts = jnp.clip(0.3 * jax.random.normal(key_shift, (LAYERS, 8, D), jnp.float32), -1.2, 1.2)
    scales = jax.random.uniform(key_scale, (LAYERS, 8, D), jnp.float32, 0.5, 1.5)
    row_kind = (jnp.arange(8) % 4)[None, :, None]
    return jnp.where(row_kind == 0, gains, jnp.where(row_kind == 3, scales, shifts))


def draw_lengths(key, part):
    key = jax.random.fold_in(key, 11)
    key_length, key_full = jax.random.split(key)
    drawn = jax.random.randint(key_length, (IMAGES,), SEQ // 4, SEQ + 1)
    chosen = jax.random.randint(key_full, (N_DP,), 0, IMG_DP)
    full_image = (jnp.arange(IMG_DP)[None, :] == chosen[:, None]).reshape(-1)
    return jnp.where(full_image, SEQ, drawn).astype(jnp.int32)


def shard_levels(stream_key, shape, pieces, smallest, largest):
    factor_of, own = 1.0, jax.random.fold_in(stream_key, 6)
    for position, parts in pieces:
        heights = jnp.exp(jax.random.uniform(jax.random.fold_in(own, position), (parts,), jnp.float32, smallest / len(pieces), largest / len(pieces)))
        factor_of = factor_of * jnp.repeat(heights, shape[position] // parts).reshape([-1 if axis == position else 1 for axis in range(len(shape))])
    return factor_of


def normal_values(key, extent, width, most, pieces=(), dtype=jnp.bfloat16):
    entries = width * jax.random.normal(key, extent, jnp.float32)
    if pieces:
        entries = entries * shard_levels(key, extent, pieces, -0.22, 0.18)
    return jnp.clip(entries, -most, most).astype(dtype)


def setup_inputs(seed: int = 0) -> dict:
    arg_keys = jax.random.split(jax.random.key(seed), 14)
    tokens = normal_values(arg_keys[0], (SEQ, IMAGES, D), 1.0, 6.0, ((0, 8), (1, 4)), jnp.float32)
    cotangent = normal_values(arg_keys[1], (SEQ, IMAGES, D), 1.0, 6.0, ((0, 8), (1, 4)), jnp.float32)
    attention_in = normal_values(arg_keys[2], (LAYERS, D, 3 * D), D ** -0.5, 0.1875, ((1, 4), (2, 8)), jnp.float32)
    attention_out = normal_values(arg_keys[3], (LAYERS, D, D), (D // 16) ** -0.5, 0.75, ((1, 4), (2, 8)), jnp.float32)
    hidden_up = normal_values(arg_keys[4], (LAYERS, D, FF), D ** -0.5, 0.1875, ((1, 4), (2, 8)), jnp.float32)
    hidden_down = normal_values(arg_keys[5], (LAYERS, D, FF), FF ** -0.5, 0.09375, ((1, 4), (2, 8)), jnp.float32)
    attention_in_momentum = draw_attention_in_momentum(jax.random.fold_in(arg_keys[13], 71), 0)
    attention_out_momentum = draw_attention_out_momentum(jax.random.fold_in(arg_keys[13], 71), 0)
    hidden_up_momentum = draw_hidden_up_momentum(jax.random.fold_in(arg_keys[13], 71), 0)
    hidden_down_momentum = draw_hidden_down_momentum(jax.random.fold_in(arg_keys[13], 71), 0)
    row_params = draw_row_params(jax.random.fold_in(arg_keys[13], 71), 0)
    column_bias = normal_values(arg_keys[11], (LAYERS, HEADS, 2 * HD + FF // HEADS), 0.3, 1.5, ((1, 8),), jnp.float32)
    lengths = draw_lengths(jax.random.fold_in(arg_keys[13], 71), 0)
    return {"tokens": tokens, "cotangent": cotangent, "attention_in": attention_in, "attention_out": attention_out, "hidden_up": hidden_up, "hidden_down": hidden_down, "attention_in_momentum": attention_in_momentum, "attention_out_momentum": attention_out_momentum, "hidden_up_momentum": hidden_up_momentum, "hidden_down_momentum": hidden_down_momentum, "row_params": row_params, "column_bias": column_bias, "lengths": lengths}


@jax.custom_vjp
def low(v):
    return lax.optimization_barrier(v.astype(jnp.bfloat16)).astype(jnp.float32)

@jax.custom_vjp
def low_back(v):
    return v

def low_keep(v):
    return (low(v), None)

def low_pass(kept, grad):
    return (grad,)

def back_keep(v):
    return (v, None)

def back_low(kept, grad):
    return (low(grad),)
low.defvjp(low_keep, low_pass)
low_back.defvjp(back_keep, back_low)
EPS_NORM = 1e-06
EPS_GRAM = 1e-07
NS_A = 3.4445
NS_B = -4.775
NS_C = 2.0315
MOMENTUM = 0.95
MUON_RATE = 0.5
SCORE_FLOOR = -1e+30
HIGHEST = lax.Precision.HIGHEST

def layer_norm(values, norm_gain, norm_shift):
    centered = values - lax.optimization_barrier(jnp.mean(values, axis=-1, keepdims=True))
    inverse = lax.rsqrt(lax.optimization_barrier(jnp.mean(centered * centered, axis=-1, keepdims=True)) + EPS_NORM)
    return centered * inverse * norm_gain + norm_shift

def attend_image(operands):
    query_rows, key_rows, value_rows, key_valid = operands
    scores = jnp.einsum('qhe,khe->hqk', query_rows, key_rows, precision=HIGHEST) * HD ** (-0.5)
    scores = low_back(scores)
    scores = jnp.where(key_valid[None, None, :], scores, SCORE_FLOOR)
    row_max = lax.optimization_barrier(jnp.max(scores, axis=-1, keepdims=True))
    exponent = jnp.exp(scores - row_max)
    softmax_rows = exponent / lax.optimization_barrier(jnp.sum(exponent, axis=-1, keepdims=True))
    return jnp.einsum('hqk,khe->qhe', low(softmax_rows), value_rows, precision=HIGHEST)

def layer_block(residual, input_weight, output_weight, up_weight, down_weight, row_set, col_set, key_valid):
    first_rows = low(layer_norm(residual, row_set[0], row_set[1]))
    projected = low_back(jnp.einsum('sid,dc->sic', first_rows, low(input_weight), precision=HIGHEST))
    projected = projected.reshape(SEQ, IMAGES, HEADS, 3, HD)
    query_rows = low(projected[:, :, :, 0] + col_set[:, :HD])
    key_rows = low(projected[:, :, :, 1])
    value_rows = low(projected[:, :, :, 2] + col_set[:, HD:2 * HD])
    head_out = lax.map(jax.checkpoint(attend_image), (jnp.moveaxis(query_rows, 1, 0), jnp.moveaxis(key_rows, 1, 0), jnp.moveaxis(value_rows, 1, 0), key_valid))
    head_rows = low_back(low(jnp.moveaxis(head_out, 0, 1).reshape(SEQ, IMAGES, D)))
    branch_one = low_back(jnp.einsum('sic,dc->sid', head_rows, low(output_weight), precision=HIGHEST)) + row_set[2]
    middle = residual + row_set[3] * branch_one
    second_rows = low(layer_norm(middle, row_set[4], row_set[5]))
    preactivation = low_back(jnp.einsum('sid,dc->sic', second_rows, low(up_weight), precision=HIGHEST)) + col_set[:, 2 * HD:].reshape(FF)
    hidden_low = low(jax.nn.gelu(preactivation, approximate=False))
    branch_two = low_back(jnp.einsum('sic,dc->sid', hidden_low, low(down_weight), precision=HIGHEST)) + row_set[6]
    return middle + row_set[7] * branch_two

def orthogonalize(moment):
    current = moment * lax.rsqrt(jnp.sum(moment * moment) + EPS_GRAM)
    for iteration in range(NS_STEPS):
        gram = jnp.dot(current, current.T, precision=HIGHEST, preferred_element_type=jnp.float32)
        polynomial = NS_B * gram + NS_C * jnp.dot(gram, gram, precision=HIGHEST, preferred_element_type=jnp.float32)
        current = NS_A * current + jnp.dot(polynomial, current, precision=HIGHEST, preferred_element_type=jnp.float32)
    return current

def muon_update(weights, momenta, grads, fan_in):
    momenta_new = MOMENTUM * momenta + grads
    ortho = jnp.stack([orthogonalize(momenta_new[block_index]) for block_index in range(LAYERS)])
    rate = MUON_RATE * math.sqrt(max(D, weights.shape[2]) / fan_in)
    return (momenta_new, weights - rate * ortho)

def reference(tokens, cotangent, attention_in, attention_out, hidden_up, hidden_down, attention_in_momentum, attention_out_momentum, hidden_up_momentum, hidden_down_momentum, row_params, column_bias, lengths):
    key_valid = lax.broadcasted_iota(jnp.int32, (IMAGES, SEQ), 1) < lengths[:, None]

    def forward(residual, input_all, output_all, up_all, down_all, rows_all, cols_all):
        for block_index in range(LAYERS):
            residual = layer_block(residual, input_all[block_index], output_all[block_index], up_all[block_index], down_all[block_index], rows_all[block_index], cols_all[block_index], key_valid)
        return residual
    layer_output, pullback = jax.vjp(forward, tokens, attention_in, attention_out, hidden_up, hidden_down, row_params, column_bias)
    tokens_grad, in_grad, out_grad, up_grad, down_grad, row_grad, column_grad = pullback(cotangent)
    in_moment, in_new = muon_update(attention_in, attention_in_momentum, in_grad, D)
    out_moment, out_new = muon_update(attention_out, attention_out_momentum, out_grad, D // 16)
    up_moment, up_new = muon_update(hidden_up, hidden_up_momentum, up_grad, D)
    down_moment, down_new = muon_update(hidden_down, hidden_down_momentum, down_grad, FF)
    small_rate = 0.3 / math.sqrt(IMAGES * SEQ)
    row_new = row_params - small_rate * row_grad
    column_new = column_bias - small_rate * column_grad
    return (layer_output, tokens_grad, in_grad, out_grad, up_grad, down_grad, in_moment, out_moment, up_moment, down_moment, in_new, out_new, up_new, down_new, row_grad, row_new, column_grad, column_new)
```

```python
import math

import jax
import jax.numpy as jnp
from jax import lax
from jax.experimental import pallas as pl
from jax.experimental.pallas import tpu as pltpu
from jax.sharding import Mesh
from jax.sharding import PartitionSpec as P

D = 1024
HD = 64
FF = 4096
NS_STEPS = 5

EPS_NORM = 1e-06
EPS_GRAM = 1e-07
NS_A = 3.4445
NS_B = -4.775
NS_C = 2.0315
MOMENTUM = 0.95
MUON_RATE = 0.5
SCORE_FLOOR = -1e30
F32 = jnp.float32
LOW = jnp.bfloat16

GROUP = ("pair", "core")
ALL = ("dp", "half", "pair", "core")
KINDS = 4


def pin(*values):
    return lax.optimization_barrier(values)


def half_swap(values):
    return lax.ppermute(values, "half", [(0, 1), (1, 0)])


def core_swap(values):
    return lax.ppermute(values, "core", [(0, 1), (1, 0)])


def pair_from(values, shift):
    count = lax.axis_size("pair")
    return lax.ppermute(values, "pair", [((i + shift) % count, i) for i in range(count)])


def from_pairs(block):
    return [pair_from(block, shift) for shift in range(1, lax.axis_size("pair"))]


def on_chips(blocks):
    return jnp.concatenate([part for block in blocks for part in (block, core_swap(block))])


def chip_sum(chunk):
    rows = chunk.shape[0] // 2
    return chunk[:rows].astype(F32) + core_swap(chunk[rows:]).astype(F32)


def far_sums(chunk):
    parts = jnp.split(chunk, lax.axis_size("pair") - 1)
    return [chip_sum(part).astype(LOW) for part in parts]


def to_pairs(sums):
    count = lax.axis_size("pair")
    return [pair_from(part, count - shift) for shift, part in enumerate(sums, 1)]


def pipelined(block, work):
    arriving = from_pairs(block)
    near = on_chips([block])
    *near_out, last = work(near)
    arriving, last = pin(arriving, last)
    total = chip_sum(last)
    far = on_chips(arriving)
    *far_out, last = work(far)
    back = to_pairs(far_sums(last))
    return (near, far), (near_out, far_out), total, back


def arrived(total, back):
    return sum((part.astype(F32) for part in back), total)


def layer_norm(values, norm_gain, norm_shift):
    centered = values - jnp.mean(values, axis=-1, keepdims=True)
    inverse = lax.rsqrt(jnp.mean(centered * centered, axis=-1, keepdims=True) + EPS_NORM)
    normed = centered * inverse
    return (normed * norm_gain + norm_shift, normed, inverse)


def norm_backward(grad_out, normed, inverse, norm_gain):
    scaled = grad_out * norm_gain
    grad_in = inverse * (
        scaled
        - jnp.mean(scaled, axis=-1, keepdims=True)
        - normed * jnp.mean(scaled * normed, axis=-1, keepdims=True)
    )
    return (grad_in, jnp.sum(grad_out * normed, axis=0), jnp.sum(grad_out, axis=0))


def dot(left, right, dims):
    return lax.dot_general(left, right, (dims, ((), ())), preferred_element_type=F32)


def times(left, right):
    return dot(left, right, ((1,), (0,)))


def times_t(left, right):
    return dot(left, right, ((1,), (1,)))


def t_times(left, right):
    return dot(left, right, ((0,), (0,)))


LANES = 128
STEP = 352

def of_head(values, head):
    lane = lax.broadcasted_iota(jnp.int32, values.shape, 1)
    return jnp.where((lane < HD) == (head == 0), values, jnp.zeros_like(values))


def attend_kernel(q_ref, kn_ref, kf_ref, vn_ref, vf_ref, bn_ref, bf_ref, out_ref, lse_ref):
    query = q_ref[...]
    low_half = lax.broadcasted_iota(jnp.int32, (query.shape[0], LANES), 1) < HD
    tops, sums = [], []
    for head in range(2):
        one = of_head(query, head)
        scores = [
            times_t(one, k_ref[...]) + b_ref[...]
            for k_ref, b_ref in ((kn_ref, bn_ref), (kf_ref, bf_ref))
        ]
        top = jnp.maximum(*[jnp.max(s, axis=1, keepdims=True) for s in scores])
        total = jnp.zeros((query.shape[0], LANES), F32)
        for s, v_ref in zip(scores, (vn_ref, vf_ref)):
            value = v_ref[...]
            lane = lax.broadcasted_iota(jnp.int32, value.shape, 1)
            value = jnp.where((lane < HD) == (head == 0), value, jnp.ones_like(value))
            total = total + times(jnp.exp(s - top).astype(LOW), value)
        tops.append(top)
        sums.append(total)
    row_sum = pltpu.roll(jnp.where(low_half, sums[1], sums[0]), HD, 1)
    out_ref[...] = (jnp.where(low_half, sums[0], sums[1]) / row_sum).astype(LOW)
    lse_ref[...] = jnp.where(low_half, tops[0], tops[1]) + jnp.log(row_sum)


def attend(query, near, far, bias_near, bias_far):
    rows, width = query.shape[0], query.shape[1] // 3
    pairs = width // LANES

    def whole(array, offset):
        return pl.BlockSpec((array.shape[0], LANES), lambda p, i: (0, 3 * p + offset))

    def full(array):
        return pl.BlockSpec(array.shape, lambda p, i: (0, 0))

    block = pl.BlockSpec((min(STEP, rows), LANES), lambda p, i: (i, p))
    query_block = pl.BlockSpec(block.block_shape, lambda p, i: (i, 3 * p))
    return pl.pallas_call(
        attend_kernel,
        out_shape=(
            jax.ShapeDtypeStruct((rows, width), LOW),
            jax.ShapeDtypeStruct((rows, width), F32),
        ),
        grid=(pairs, pl.cdiv(rows, STEP)),
        in_specs=[
            query_block,
            whole(near, 1),
            whole(far, 1),
            whole(near, 2),
            whole(far, 2),
            full(bias_near),
            full(bias_far),
        ],
        out_specs=(block, block),
        compiler_params=pltpu.CompilerParams(vmem_limit_bytes=48 * 2**20),
        name="attend",
    )(query, near, far, near, far, bias_near, bias_far)


def attend_back_kernel(
    q_ref, k_ref, v_ref, bias_ref, do_ref, out_ref, lse_ref,
    grad_ref, sum_ref,
    lse_row, delta_row, dq_acc, sum_acc,
):
    step, steps = pl.program_id(1), pl.num_programs(1)
    block = k_ref.shape[0]
    query, grad = q_ref[...], do_ref[...]

    @pl.when(step == 0)
    def _():
        lse_row[...] = jnp.transpose(lse_ref[...])
        delta_row[...] = jnp.transpose(grad.astype(F32) * out_ref[...].astype(F32))
        dq_acc[...] = jnp.zeros_like(dq_acc)
        sum_acc[...] = jnp.zeros_like(sum_acc)

    key, value = k_ref[...], v_ref[...]
    key_turned = jnp.transpose(key.astype(F32)).astype(LOW)
    grad_key = jnp.zeros((block, LANES), F32)
    grad_value = jnp.zeros((block, LANES), F32)
    for head in range(2):
        lanes = pl.ds(head * HD, HD)
        query_one, grad_one = of_head(query, head), of_head(grad, head)
        soft = jnp.exp(times_t(key, query_one) + bias_ref[...] - lse_row[pl.ds(head * HD, 1), :])
        delta = jnp.sum(delta_row[lanes, :], axis=0, keepdims=True)
        slope = (soft * (times_t(value, grad_one) - delta)).astype(LOW)
        grad_value += times(soft.astype(LOW), grad_one)
        grad_key += times(slope, query_one)
        dq_acc[lanes, :] += times(key_turned[head * HD : (head + 1) * HD], slope)
    rows = pl.ds(pl.multiple_of(step * block, 16), block)
    grad_ref[rows, LANES : 2 * LANES] = grad_key.astype(LOW)
    grad_ref[rows, 2 * LANES :] = grad_value.astype(LOW)
    sum_acc[1:2, :] += jnp.sum(grad_value, axis=0, keepdims=True)

    @pl.when(step == steps - 1)
    def _():
        grad_query = jnp.transpose(dq_acc[...]) * HD**-0.5
        grad_ref[:, :LANES] = grad_query.astype(LOW)
        sum_acc[0:1, :] = jnp.sum(grad_query, axis=0, keepdims=True)
        sum_ref[...] = sum_acc[...]


def attend_back(projected, bias, grad_out, out, lse):
    rows, width = out.shape
    pairs, step = width // LANES, rows // 2

    def whole(scale):
        return pl.BlockSpec((rows, LANES), lambda p, i: (0, scale * p))

    def part(offset):
        return pl.BlockSpec((step, LANES), lambda p, i: (i, 3 * p + offset))

    return pl.pallas_call(
        attend_back_kernel,
        out_shape=(
            jax.ShapeDtypeStruct((rows, 3 * width), LOW),
            jax.ShapeDtypeStruct((8, width), F32),
        ),
        grid=(pairs, 2),
        in_specs=[
            whole(3),
            part(1),
            part(2),
            pl.BlockSpec((step, 1), lambda p, i: (i, 0)),
            whole(1),
            whole(1),
            whole(1),
        ],
        out_specs=(
            pl.BlockSpec((rows, 3 * LANES), lambda p, i: (0, p)),
            pl.BlockSpec((8, LANES), lambda p, i: (0, p)),
        ),
        scratch_shapes=[
            pltpu.VMEM((LANES, rows), F32),
            pltpu.VMEM((LANES, rows), F32),
            pltpu.VMEM((LANES, rows), F32),
            pltpu.VMEM((8, LANES), F32),
        ],
        compiler_params=pltpu.CompilerParams(vmem_limit_bytes=56 * 2**20),
        name="attend_back",
    )(projected, projected, projected, bias, grad_out, out, lse)


UNITS = 256


def gelu_and_slope(values):
    size = jnp.abs(values)
    inner = 1.0 / (1.0 + (0.3275911 * 0.5**0.5) * size)
    tail = 0.5 * 1.061405429
    for term in (-1.453152027, 1.421413741, -0.284496736, 0.254829592):
        tail = tail * inner + 0.5 * term
    bell = jnp.exp(-0.5 * values * values)
    tail = tail * inner * bell
    share = jnp.where(values < 0, tail, 1.0 - tail)
    return values * share, share + values * ((2 * math.pi) ** -0.5 * bell)


def hidden_kernel(rows_ref, own_up, own_down, far_up, far_down, bias_ref, low_ref, slope_ref, out_ref, total):
    step, steps = pl.program_id(0), pl.num_programs(0)

    @pl.when(step == 0)
    def _():
        total[...] = jnp.zeros_like(total)

    def work(up_ref, down_ref):
        value, slope = gelu_and_slope(times(rows_ref[...], up_ref[...]) + bias_ref[...])
        value = value.astype(LOW)
        low_ref[...] = value
        slope_ref[...] = slope.astype(LOW)
        total[...] += times_t(value, down_ref[...])

    @pl.when(step < steps // 2)
    def _():
        work(own_up, own_down)

    @pl.when(step >= steps // 2)
    def _():
        work(far_up, far_down)

    @pl.when(step == steps - 1)
    def _():
        out_ref[...] = total[...].astype(LOW)


def hidden_back_kernel(grad_ref, own_up, own_down, far_up, far_down, slope_ref, pre_ref, sum_ref, out_ref, total):
    step, steps = pl.program_id(0), pl.num_programs(0)

    @pl.when(step == 0)
    def _():
        total[...] = jnp.zeros_like(total)

    def work(up_ref, down_ref):
        grad_pre = times(grad_ref[...], down_ref[...]) * slope_ref[...].astype(F32)
        sum_ref[...] = jnp.broadcast_to(jnp.sum(grad_pre, axis=0, keepdims=True), sum_ref.shape)
        grad_pre = grad_pre.astype(LOW)
        pre_ref[...] = grad_pre
        total[...] += times_t(grad_pre, up_ref[...])

    @pl.when(step < steps // 2)
    def _():
        work(own_up, own_down)

    @pl.when(step >= steps // 2)
    def _():
        work(far_up, far_down)

    @pl.when(step == steps - 1)
    def _():
        out_ref[...] = total[...].astype(LOW)


def hidden_call(kernel, rows_in, sides, units, extra, extra_spec, outs, name):
    rows, width = rows_in.shape
    steps = units // UNITS
    half_steps = steps // 2
    block = pl.BlockSpec((rows, UNITS), lambda j: (0, j))
    whole = pl.BlockSpec((rows, width), lambda j: (0, 0))

    def part(at, begin):
        return pl.BlockSpec(
            (width, UNITS),
            lambda j: (0, at // UNITS + jnp.clip(j - begin, 0, half_steps - 1)),
        )

    specs, arrays = [], []
    for side, (array, at) in enumerate(sides):
        specs += [part(at, side * half_steps), part(at + units // 2, side * half_steps)]
        arrays += [array, array]
    return pl.pallas_call(
        kernel,
        out_shape=tuple(shape for shape, _ in outs),
        grid=(steps,),
        in_specs=[whole, *specs, extra_spec or block],
        out_specs=tuple(spec or block for _, spec in outs),
        scratch_shapes=[pltpu.VMEM((rows, width), F32)],
        compiler_params=pltpu.CompilerParams(vmem_limit_bytes=48 * 2**20),
        name=name,
    )(rows_in, *arrays, extra)


def hidden_layer(rows_in, sides, bias):
    rows, width = rows_in.shape
    units = jax.ShapeDtypeStruct((rows, bias.shape[1]), LOW)
    return hidden_call(
        hidden_kernel,
        rows_in,
        sides,
        bias.shape[1],
        bias,
        pl.BlockSpec((1, UNITS), lambda j: (0, j)),
        [
            (units, None),
            (units, None),
            (
                jax.ShapeDtypeStruct((rows, width), LOW),
                pl.BlockSpec((rows, width), lambda j: (0, 0)),
            ),
        ],
        "hidden_layer",
    )


def hidden_back(grad, sides, slope):
    rows, width = grad.shape
    grad_pre, total, out = hidden_call(
        hidden_back_kernel,
        grad,
        sides,
        slope.shape[1],
        slope,
        None,
        [
            (jax.ShapeDtypeStruct(slope.shape, LOW), None),
            (
                jax.ShapeDtypeStruct((8, slope.shape[1]), F32),
                pl.BlockSpec((8, UNITS), lambda j: (0, j)),
            ),
            (
                jax.ShapeDtypeStruct((rows, width), LOW),
                pl.BlockSpec((rows, width), lambda j: (0, 0)),
            ),
        ],
        "hidden_back",
    )
    return grad_pre, total[0], out


def gram_sum(partial, axes, aside):
    middle, quarter = partial.shape[0] // 2, partial.shape[0] // 4
    first_block, side_block = partial[:middle, :middle], partial[:middle, middle:]
    last_block = partial[middle:, middle:]
    if lax.axis_size("pair") != 2 or len(axes) > len(GROUP):
        return pin(lax.psum((first_block, side_block, last_block), axes), aside)
    first = lax.axis_index("core") == 0
    upper = jnp.concatenate([first_block, side_block[:quarter]])
    lower = jnp.concatenate([last_block, side_block[quarter:]])
    mine = jnp.where(first, upper, lower) + core_swap(jnp.where(first, lower, upper))
    far, aside = pin(pair_from(mine, 1), aside)
    mine = mine + far
    other = core_swap(mine)
    upper, lower = jnp.where(first, mine, other), jnp.where(first, other, mine)
    side_block = jnp.concatenate([upper[middle:], lower[middle:]])
    return (upper[:middle], side_block, lower[:middle]), aside


def sum_over(values, axes):
    for axis in axes:
        count, bit = lax.axis_size(axis), 1
        while bit < count:
            values = values + lax.ppermute(values, axis, [(i, i ^ bit) for i in range(count)])
            bit *= 2
    return values


def gram_of(matrix):
    low = matrix.astype(LOW)
    return times_t(low, low)


CHUNK = 256


def newton_schulz_kernel(
    first_ref, side_ref, last_ref, start_ref, out_ref,
    gram, poly, turn, gram_rest, poly_rest, turn_rest, current, current_low,
    gram_col, poly_col, turn_col, gram_row, poly_row,
):
    middle = first_ref.shape[0]
    chunks = 2 * middle // CHUNK
    gram[:middle, :middle] = first_ref[...]
    gram[:middle, middle:] = side_ref[...]
    gram[middle:, :middle] = jnp.transpose(side_ref[...])
    gram[middle:, middle:] = last_ref[...]
    on = lax.broadcasted_iota(jnp.int32, (CHUNK, CHUNK), 0) == lax.broadcasted_iota(
        jnp.int32, (CHUNK, CHUNK), 1
    )

    def part(i):
        return pl.ds(pl.multiple_of(i * CHUNK, CHUNK), CHUNK)

    def each(work):
        def step(i, carry):
            work(part(i))
            return carry

        lax.fori_loop(0, chunks, step, 0)

    def keep(rows, value, excess, whole, rest, col, row):
        whole[rows, :] = value
        rest[rows, :] = value.astype(LOW)
        block = whole[rows, rows] - jnp.where(on, excess, 0.0)
        whole[rows, rows] = block
        rest[rows, rows] = jnp.where(on, 0.0, block).astype(LOW)
        diagonal = jnp.where(on, block, 0.0)
        col[rows, :] = jnp.sum(diagonal, axis=1, keepdims=True)
        if row is not None:
            row[:, rows] = jnp.sum(diagonal, axis=0, keepdims=True)

    def product(rows, left, left_rest, left_col, right, right_rest, right_row):
        return (
            times(left_rest[rows, :], right_rest[...])
            + left_col[rows, :] * right[rows, :]
            + left[rows, :] * right_row[...]
        )

    trace = jnp.zeros((1, 1), F32)
    for i in range(chunks):
        at = slice(i * CHUNK, (i + 1) * CHUNK)
        diagonal = jnp.where(on, gram[at, at], 0.0)
        trace += jnp.sum(jnp.sum(diagonal, axis=1, keepdims=True), axis=0, keepdims=True)
    inverse = lax.rsqrt(trace + EPS_GRAM)

    def begin(rows):
        scaled = gram[rows, :] * (inverse * inverse)
        keep(rows, scaled, 0.0, gram, gram_rest, gram_col, gram_row)
        value = start_ref[rows, :] * inverse
        current[rows, :] = value
        current_low[0, rows, :] = value.astype(LOW)

    each(begin)

    def polynomial(rows):
        square = product(rows, gram, gram_rest, gram_col, gram, gram_rest, gram_row)
        excess = NS_C * gram_col[rows, :] * gram_col[rows, :]
        value = NS_B * gram[rows, :] + NS_C * square
        keep(rows, value, excess, poly, poly_rest, poly_col, poly_row)

    def advanced(rows, slot):
        moved = times(poly_rest[rows, :], current_low[slot])
        return (NS_A + poly_col[rows, :]) * current[rows, :] + moved

    def iterate(iteration, carry):
        slot = lax.rem(iteration, 2)
        each(polynomial)

        def advance(rows):
            value = advanced(rows, slot)
            current[rows, :] = value
            current_low[1 - slot, rows, :] = value.astype(LOW)

        each(advance)

        def first(rows):
            value = product(rows, poly, poly_rest, poly_col, gram, gram_rest, gram_row)
            excess = poly_col[rows, :] * gram_col[rows, :]
            keep(rows, NS_A * gram[rows, :] + value, excess, turn, turn_rest, turn_col, None)

        each(first)

        def second(rows):
            value = product(rows, turn, turn_rest, turn_col, poly, poly_rest, poly_row)
            excess = turn_col[rows, :] * poly_col[rows, :]
            keep(rows, NS_A * turn[rows, :] + value, excess, gram, gram_rest, gram_col, gram_row)

        each(second)
        return carry

    lax.fori_loop(0, NS_STEPS - 1, iterate, 0)
    each(polynomial)

    def finish(rows):
        out_ref[rows, :] = advanced(rows, (NS_STEPS - 1) % 2).astype(LOW)

    each(finish)


def orthogonalize(start, gram):
    size, width = start.shape
    square = [pltpu.VMEM((size, size), F32)] * 3 + [pltpu.VMEM((size, size), LOW)] * 3
    return pl.pallas_call(
        newton_schulz_kernel,
        out_shape=jax.ShapeDtypeStruct((size, width), LOW),
        in_specs=[pl.BlockSpec(memory_space=pltpu.VMEM)] * 4,
        out_specs=pl.BlockSpec(memory_space=pltpu.VMEM),
        scratch_shapes=square
        + [pltpu.VMEM((size, width), F32), pltpu.VMEM((2, size, width), LOW)]
        + [pltpu.VMEM((size, 1), F32)] * 3
        + [pltpu.VMEM((1, size), F32)] * 2,
        compiler_params=pltpu.CompilerParams(vmem_limit_bytes=56 * 2**20),
        name="newton_schulz",
    )(*gram, start)


def per_device(
    tokens,
    cotangent,
    attention_in,
    attention_out,
    hidden_up,
    hidden_down,
    attention_in_momentum,
    attention_out_momentum,
    hidden_up_momentum,
    hidden_down_momentum,
    row_params,
    column_bias,
    lengths,
):
    local_rows, image_count, _ = tokens.shape
    pair_count = lax.axis_size("pair")
    data_count = lax.axis_size("dp")
    half = lax.axis_index("half")
    layer_count = attention_in.shape[0]
    rows_owned = hidden_up.shape[1]
    head_own = column_bias.shape[1]
    heads = 2 * head_own
    head_width = heads * HD
    seq_total = local_rows * 4 * pair_count

    def away(values):
        own = jnp.where(half == 0, values[:, 0], values[:, 1])
        return own, jnp.where(half == 0, values[:, 1], values[:, 0]).astype(LOW)

    def together(own, other):
        return jnp.concatenate([own, other.astype(F32)], axis=0)

    def at_home(own, other):
        other = other.astype(F32)
        return jnp.where(
            half == 0, jnp.stack([own, other], axis=1), jnp.stack([other, own], axis=1)
        )

    place = []
    for shift in range(pair_count):
        chip = lax.rem(lax.axis_index("pair") + shift, pair_count)
        for flip in range(2):
            core = lax.axis_index("core") ^ flip
            for other in range(2):
                block = ((half ^ other) * pair_count + chip) * 2 + core
                place.append(block * local_rows + jnp.arange(local_rows, dtype=jnp.int32))
    length = jnp.where(half == 0, lengths[0], lengths[1])
    key_bias = jnp.where(jnp.concatenate(place) < length, 0.0, SCORE_FLOOR).astype(F32)
    near_rows = 4 * local_rows
    bias_near, bias_far = key_bias[None, :near_rows], key_bias[None, near_rows:]

    column_other = half_swap(column_bias)
    column_all = jnp.concatenate([column_bias, column_other], axis=1)
    data_index = lax.axis_index("dp")
    kinds = range(KINDS)
    side_width = 3 * head_own * HD
    by_side = head_own * HD == LANES
    matrix_count = layer_count * KINDS
    wide = data_count * 2 == matrix_count
    pad_width = hidden_up.shape[2]
    column_axes = GROUP if wide else GROUP + ("half",)

    def dp_xor(values, offset):
        return lax.ppermute(values, "dp", [(i, i ^ offset) for i in range(data_count)])

    def data_gather(piece):
        return lax.all_gather(piece, "dp", axis=0, tiled=True)

    def data_sum(partial):
        return lax.psum_scatter(partial, "dp", scatter_dimension=0, tiled=True)

    def sides(own, other):
        if not by_side:
            own, other = (w.reshape(-1, 3, head_own * HD) for w in (own, other))
        return jnp.concatenate([own, other], axis=-1).reshape(own.shape[0], 2 * side_width)

    def own_weights(block_index):
        first = attention_in[block_index].astype(LOW).reshape(rows_owned, head_own, 3, HD)
        first = jnp.swapaxes(first, 1, 2).reshape(rows_owned, -1)
        return (
            jnp.concatenate([first, attention_out[block_index].astype(LOW)], axis=1),
            jnp.concatenate(
                [hidden_up[block_index].astype(LOW), hidden_down[block_index].astype(LOW)], axis=1
            ),
        )

    def attention_matrices(own, other):
        return (
            sides(own[:, :side_width], other[:, :side_width]),
            jnp.concatenate([own[:, side_width:], other[:, side_width:]], axis=1),
        )

    moments_old = (
        attention_in_momentum,
        attention_out_momentum,
        hidden_up_momentum,
        hidden_down_momentum,
    )

    def padded(array):
        return jnp.pad(array, ((0, 0), (0, pad_width - array.shape[1])))

    def moment_away():
        first, second = (
            jnp.concatenate([m[layer] for m in moments_old], axis=1).astype(LOW)
            for layer in range(2)
        )
        return jnp.where(half == 0, first, second), jnp.where(half == 0, second, first)

    def moment_items(own, other):
        items, at = [], 0
        for kind, moment in enumerate(moments_old):
            width = moment.shape[2]
            if wide:
                pair = [padded(array[:, at : at + width]) for array in (own, other)]
                items.append((kind, jnp.concatenate(pair, axis=1)))
            else:
                items += [
                    (l * KINDS + kind, padded(moment[l].astype(LOW))) for l in range(layer_count)
                ]
            at += width
        return items

    def to_owner(items):
        stack = jnp.stack([rows for _, rows in sorted(items, key=lambda item: item[0])])
        blocks = []
        for offset in range(data_count):
            block = lax.dynamic_index_in_dim(stack, data_index ^ offset, 0, keepdims=False)
            blocks.append(dp_xor(block, offset) if offset else block)
        return blocks

    def from_owner(matrix):
        blocks = jnp.split(matrix, data_count)

        def gathered(parts):
            return [
                lax.dynamic_index_in_dim(jnp.stack(parts), data_index ^ owner, 0, keepdims=False)
                for owner in range(data_count)
            ]

        if not wide:
            parts = gathered([dp_xor(b, i) if i else b for i, b in enumerate(blocks)])
            return [parts[layer * KINDS : (layer + 1) * KINDS] for layer in range(layer_count)]
        far, near = [], []
        for offset, block in enumerate(blocks):
            pairs = [
                (2 * i + h, 2 * (i ^ offset) + 1 - h) for i in range(data_count) for h in range(2)
            ]
            far.append(lax.ppermute(block[:, pad_width:], ("dp", "half"), pairs))
        for offset, block in enumerate(blocks):
            near.append(
                dp_xor(block[:, :pad_width], offset) if offset else block[:, :pad_width]
            )
        near, far = gathered(near), gathered(far)
        return [
            [jnp.where(half == layer, n, f) for n, f in zip(near, far)]
            for layer in range(layer_count)
        ]

    own_low = [own_weights(block_index) for block_index in range(layer_count)]
    params = row_params
    part_of = jnp.arange(3 * head_width) % (3 * LANES) // LANES
    query_scale = jnp.where(part_of == 0, HD**-0.5, 1.0).astype(LOW)
    own_tokens, other_tokens = away(tokens)
    other_tokens = half_swap(other_tokens)
    first_own = data_gather(own_low[0][0])
    first_other = half_swap(own_low[0][0])
    first_own, first_other, own = pin(first_own, first_other, own_low[0][1])
    first_other = data_gather(first_other)
    hidden_other = half_swap(own)
    hidden_own = data_gather(own)
    residual = together(own_tokens, other_tokens)
    kept = []

    for block_index in range(layer_count):
        last = block_index == layer_count - 1
        row_set = params[block_index]
        col_set = column_all[block_index]
        unit_bias = col_set[:, 2 * HD :].reshape(1, -1)
        query_bias = col_set[:, :HD].reshape(-1, LANES)
        value_bias = col_set[:, HD : 2 * HD].reshape(-1, LANES)
        in_bias = jnp.concatenate(
            [query_bias, jnp.zeros_like(query_bias), value_bias], axis=1
        ).reshape(-1)
        norm_one, normed_first, inverse_first = layer_norm(residual, row_set[0], row_set[1])
        block = norm_one.astype(LOW)
        arriving = from_pairs(block)
        near = on_chips([block])
        w_in, w_out = attention_matrices(first_own, first_other)

        def project(rows):
            return (times(rows, w_in) + in_bias).astype(LOW) * query_scale

        query_near = project(near)
        if block_index > 0:
            query_near, own = pin(query_near, own_low[block_index][1])
            hidden_other = half_swap(own)
            hidden_own = data_gather(own)
        arriving, query_near = pin(arriving, query_near)
        far = on_chips(arriving)
        query_far = project(far)
        heads_far, lse_far = attend(query_far, query_near, query_far, bias_near, bias_far)
        if last:
            heads_far, hidden_other, (own_cotangent, other) = pin(
                heads_far, hidden_other, away(cotangent)
            )
            aside = half_swap(other)
        else:
            heads_far, hidden_other, first_own = pin(
                heads_far, hidden_other, own_low[block_index + 1][0]
            )
            aside = half_swap(first_own)
            first_own = data_gather(first_own)
        hidden_other = data_gather(hidden_other)
        sums, query_held = pin(far_sums(times_t(heads_far, w_out).astype(LOW)), query_near)
        back = to_pairs(sums)
        heads_near, lse_near = attend(query_held, query_near, query_far, bias_near, bias_far)
        heads_near, back, aside = pin(heads_near, back, aside)
        if last:
            other_cotangent = aside
        else:
            first_other = data_gather(aside)
        total = chip_sum(times_t(heads_near, w_out).astype(LOW))
        branch_one = arrived(total, back) + row_set[2]
        middle = residual + row_set[3] * branch_one
        norm_two, normed_second, inverse_second = layer_norm(middle, row_set[4], row_set[5])
        hidden_full = ((hidden_own, 0), (hidden_other, 0))
        second, second_out, total, back = pipelined(
            norm_two.astype(LOW),
            lambda rows: hidden_layer(rows, hidden_full, unit_bias),
        )
        branch_two = arrived(total, back) + row_set[6]
        residual = middle + row_set[7] * branch_two
        kept.append(
            (
                (w_in, w_out, hidden_full),
                normed_first,
                inverse_first,
                jnp.concatenate([near, far]),
                jnp.concatenate([query_near, query_far]),
                jnp.concatenate([lse_near, lse_far]),
                jnp.concatenate([heads_near, heads_far]),
                branch_one,
                normed_second,
                inverse_second,
                second,
                second_out,
                branch_two,
            )
        )
    grad_residual = together(own_cotangent, other_cotangent)

    row_terms = [None] * layer_count
    column_terms = [None] * layer_count
    owner_layers = [[None] * layer_count for _ in kinds]

    def to_half(reduced, layer):
        width = reduced.shape[1] // 2
        swapped = jnp.concatenate([reduced[:, width:], reduced[:, :width]], axis=1)
        return reduced, lax.ppermute(swapped, "half", [(1 - layer, layer)])

    def attention_grads(rows_in, rows_out, grad_proj, head_rows):
        in_grad, out_grad = t_times(rows_in, grad_proj), t_times(rows_out, head_rows)
        if not by_side:
            in_grad = in_grad.reshape(D, 3, 2, head_own * HD).transpose(0, 2, 1, 3).reshape(D, -1)
        first, second = jnp.split(in_grad, 2, axis=1), jnp.split(out_grad, 2, axis=1)
        return jnp.concatenate([first[0], second[0], first[1], second[1]], axis=1).astype(LOW)

    def settle(layer, both, part):
        full = both[0].astype(F32) + both[1].astype(F32)
        own, other = jnp.split(full, 2, axis=1)
        if part == "attention":
            owner_layers[0][layer] = (own[:, :side_width], other[:, :side_width])
            owner_layers[1][layer] = (own[:, side_width:], other[:, side_width:])
        else:
            owner_layers[part][layer] = (own, other)

    def heads_first(array):
        return jnp.swapaxes(array.reshape(-1, 3, head_own, HD), 1, 2).reshape(array.shape)

    def give_back(layer, owned):
        sent = jnp.concatenate([owned[k][layer][1].astype(LOW) for k in kinds], axis=1)
        return lax.ppermute(sent, "half", [(layer, 1 - layer)])

    def home_grads(layer, arrived_low):
        grads, at = [], 0
        for kind in kinds:
            own = owner_layers[kind][layer][0]
            width = own.shape[1]
            own = jnp.where(half == layer, own, arrived_low[:, at : at + width].astype(F32))
            at += width
            grads.append(heads_first(own) if kind == 0 else own)
        return grads

    def owner_items(kind):
        pair = [
            jnp.where(half == 0, first, second).astype(LOW)
            for first, second in zip(*owner_layers[kind])
        ]
        if kind == 0:
            pair = [heads_first(part) for part in pair]
        return [(kind, jnp.concatenate([padded(part) for part in pair], axis=1))]

    top = layer_count - 1
    for block_index in reversed(range(layer_count)):
        last = block_index == top
        (
            (w_in, w_out, hidden_full),
            normed_first,
            inverse_first,
            first,
            projected,
            lse,
            head_rows,
            branch_one,
            normed_second,
            inverse_second,
            second,
            second_out,
            branch_two,
        ) = kept[block_index]
        row_set = params[block_index]
        near_rows = 4 * local_rows
        grad_two = grad_residual * row_set[7]
        slopes = iter([chunk[1] for chunk in second_out])
        reach, back_out, total, back = pipelined(
            grad_two.astype(LOW),
            lambda rows: hidden_back(rows, hidden_full, next(slopes)),
        )
        scale_two = jnp.sum(grad_residual * branch_two, axis=0)
        shift_down = jnp.sum(grad_two, axis=0)
        unit_grad = sum(chunk[1] for chunk in back_out)
        down_grad = t_times(jnp.concatenate(reach), jnp.concatenate([c[0] for c in second_out]))
        back, down_grad = pin(back, down_grad.astype(LOW))
        if not last:
            down_sum = data_sum(down_grad)
            back, sums_late = pin(back, jnp.split(sums_late, 3))
            down_late = to_half(sums_late[0], top)
        grad_norm = arrived(total, back)
        grad_in, gain_two, shift_two = norm_backward(
            grad_norm, normed_second, inverse_second, row_set[4]
        )
        grad_residual = grad_residual + grad_in

        grad_one = grad_residual * row_set[3]
        block = grad_one.astype(LOW)
        arriving = from_pairs(block)
        scale_one = jnp.sum(grad_residual * branch_one, axis=0)
        shift_out = jnp.sum(grad_one, axis=0)
        near = on_chips([block])
        heads_near = times(near, w_out).astype(LOW)
        up_grad = t_times(jnp.concatenate(second), jnp.concatenate([c[0] for c in back_out]))
        arriving, heads_near, up_grad = pin(arriving, heads_near, up_grad.astype(LOW))
        if not last:
            heads_near, down_late = pin(heads_near, down_late)
            settle(top, down_late, 3)
            up_late = to_half(sums_late[1], top)
        far = on_chips(arriving)
        grad_heads = jnp.concatenate([heads_near, times(far, w_out).astype(LOW)])
        if not last:
            up_sum = data_sum(up_grad)
            grad_heads, down_sum = pin(grad_heads, down_sum)
            down_half = to_half(down_sum, block_index)
        if last:
            grad_heads, (own_moment, away_moment) = pin(grad_heads, moment_away())
            other_moment = half_swap(away_moment)
        else:
            grad_heads, own_moment, other_moment = pin(grad_heads, own_moment, other_moment)
            owner_moment = to_owner(moment_items(own_moment, other_moment))
        grad_proj, head_sums = attend_back(projected, key_bias[:, None], grad_heads, head_rows, lse)
        if last:
            grad_proj, other_moment, residual = pin(grad_proj, other_moment, residual)
            output_other = half_swap(residual[local_rows:].astype(LOW))
        else:
            grad_proj, owner_moment, up_late, down_half, up_sum = pin(
                grad_proj, owner_moment, up_late, down_half, up_sum
            )
            up_half = to_half(up_sum, block_index)
            settle(top, up_late, 2)
            attention_late = to_half(sums_late[2], top)
        reach = jnp.concatenate([near, far])
        if not last:
            attention_low = attention_grads(first, reach, grad_proj, head_rows)
            attention_low, grad_proj = pin(attention_low, grad_proj)
            attention_sum = data_sum(attention_low)
        sums, (grad_proj, reach, head_rows, first) = pin(
            far_sums(times_t(grad_proj[near_rows:], w_in).astype(LOW)),
            (grad_proj, reach, head_rows, first),
        )
        back = to_pairs(sums)
        total = chip_sum(times_t(grad_proj[:near_rows], w_in).astype(LOW))
        if last:
            attention_low = attention_grads(first, reach, grad_proj, head_rows)
            blocks = zip(*[jnp.split(g, data_count) for g in (down_grad, up_grad, attention_low)])
            sums_late = data_sum(jnp.concatenate([g for block in blocks for g in block]))
            back, total, attention_low, output_other = pin(back, total, attention_low, output_other)
            layer_output = at_home(residual[:local_rows], output_other)
        else:
            settle(block_index, down_half, 3)
            total, attention_late, up_half = pin(total, attention_late, up_half)
            settle(top, attention_late, "attention")
            settle(block_index, up_half, 2)
            total, attention_sum = pin(total, attention_sum)
            attention_half = to_half(attention_sum, 0)
            back, total = pin(back, total)
        grad_norm = sum((part.astype(F32) for part in back), total)
        grad_in, gain_one, shift_one = norm_backward(
            grad_norm, normed_first, inverse_first, row_set[0]
        )
        grad_residual = grad_residual + grad_in
        row_terms[block_index] = jnp.stack(
            [
                gain_one,
                shift_one,
                shift_out,
                scale_one,
                gain_two,
                shift_two,
                shift_down,
                scale_two,
            ]
        )
        column_terms[block_index] = jnp.concatenate(
            [
                head_sums[0].reshape(heads, HD),
                head_sums[1].reshape(heads, HD),
                unit_grad.reshape(heads, -1),
            ],
            axis=1,
        )
    settle(0, attention_half, "attention")
    if wide:
        owner_grad = to_owner([item for kind in kinds for item in owner_items(kind)])
        owner_grad, owner_layers, grad_residual, row_terms, column_terms = pin(
            owner_grad, owner_layers, grad_residual, row_terms, column_terms
        )
    else:
        grads = [home_grads(layer, give_back(layer, owner_layers)) for layer in range(layer_count)]
        owner_grad = to_owner(
            [
                (layer * KINDS + kind, padded(grads[layer][kind].astype(LOW)))
                for layer in range(layer_count)
                for kind in kinds
            ]
        )
    start = jnp.concatenate(
        [MOMENTUM * m.astype(F32) + g.astype(F32) for m, g in zip(owner_moment, owner_grad)]
    )
    gram_part = gram_of(start)
    grad_residual, row_terms, column_terms, gram_part = pin(
        grad_residual, row_terms, column_terms, gram_part
    )
    columns = jnp.stack(column_terms)
    flat = jnp.pad(columns.reshape(-1), (0, -columns.size % D)).reshape(-1, D)
    small = sum_over(jnp.concatenate([jnp.stack(row_terms).reshape(-1, D), flat]), ("dp",))
    rows_small = 8 * layer_count
    columns = small[rows_small:].reshape(-1)[: columns.size].reshape(columns.shape)
    owned_width = column_bias.shape[2] // data_count
    columns = lax.dynamic_slice_in_dim(columns, data_index * owned_width, owned_width, 2)
    column_grad = columns[:, :head_own] + half_swap(columns[:, head_own:])
    row_grad = sum_over(small[:rows_small], ("core", "pair", "half")).reshape(row_params.shape)
    gram, (row_grad, column_grad) = gram_sum(gram_part, column_axes, (row_grad, column_grad))
    tokens_other = grad_residual[local_rows:].astype(LOW)
    gram, row_grad, column_grad, tokens_other, owner_layers = pin(
        gram, row_grad, column_grad, tokens_other, owner_layers
    )
    tokens_other = half_swap(tokens_other)
    returning = [give_back(layer, owner_layers) for layer in range(layer_count)] if wide else []
    finish, returning, tokens_other = pin(orthogonalize(start, gram), returning, tokens_other)
    returned = from_owner(finish)
    if wide:
        grads = [home_grads(layer, arrived_low) for layer, arrived_low in enumerate(returning)]
    tokens_grad = at_home(grad_residual[:local_rows], tokens_other)
    grads = [jnp.stack(layers) for layers in zip(*grads)]
    moments = [MOMENTUM * m + g for m, g in zip(moments_old, grads)]
    olds = (attention_in, attention_out, hidden_up, hidden_down)
    fans = (D, D // 16, D, FF)
    news = []
    for kind in range(KINDS):
        width = olds[kind].shape[2]
        rate = MUON_RATE * math.sqrt(max(D, width * 4 * pair_count) / fans[kind])
        step = jnp.stack([returned[layer][kind][:, :width] for layer in range(layer_count)])
        news.append(olds[kind] - rate * step.astype(F32))
    small_rate = 0.3 / math.sqrt(image_count * data_count * seq_total)
    row_new = row_params - small_rate * row_grad
    owned_width = column_grad.shape[2]
    column_old = lax.dynamic_slice_in_dim(
        column_bias, lax.axis_index("dp") * owned_width, owned_width, 2
    )
    column_new = column_old - small_rate * column_grad
    return (
        layer_output,
        tokens_grad,
        *grads,
        *moments,
        *news,
        row_grad,
        row_new,
        column_grad,
        column_new,
    )


def solution(mesh):
    data_count, tensor_count = mesh.shape["dp"], mesh.shape["tensor"]
    cut = Mesh(mesh.devices.reshape(data_count, 2, tensor_count // 4, 2), ALL)
    tensor = ("half", "pair", "core")
    token_spec = P(tensor, "dp", None)
    matrix_spec = P(None, "dp", tensor)
    in_specs = (
        (token_spec,) * 2 + (matrix_spec,) * 8 + (P(), P(None, tensor, None), P("dp"))
    )
    out_specs = (
        (token_spec,) * 2 + (matrix_spec,) * 12 + (P(), P()) + (P(None, tensor, "dp"),) * 2
    )
    return jax.shard_map(
        per_device, mesh=cut, in_specs=in_specs, out_specs=out_specs, check_vma=False
    )
```

```python
import math

import jax
import jax.numpy as jnp
from jax import lax
from jax.experimental import pallas as pl
from jax.experimental.pallas import tpu as pltpu
from jax.sharding import Mesh
from jax.sharding import PartitionSpec as P

D = 1024
HD = 64
FF = 4096
NS_STEPS = 5

EPS_NORM = 1e-06
EPS_GRAM = 1e-07
NS_A = 3.4445
NS_B = -4.775
NS_C = 2.0315
MOMENTUM = 0.95
MUON_RATE = 0.5
SCORE_FLOOR = -1e30
F32 = jnp.float32
LOW = jnp.bfloat16

GROUP = ("pair", "core")
ALL = ("dp", "half", "pair", "core")
KINDS = 4


def pin(*values):
    return lax.optimization_barrier(values)


def half_swap(values):
    return lax.ppermute(values, "half", [(0, 1), (1, 0)])


def core_swap(values):
    return lax.ppermute(values, "core", [(0, 1), (1, 0)])


def pair_from(values, shift):
    count = lax.axis_size("pair")
    return lax.ppermute(values, "pair", [((i + shift) % count, i) for i in range(count)])


def from_pairs(block):
    return [pair_from(block, shift) for shift in range(1, lax.axis_size("pair"))]


def on_chips(blocks):
    return jnp.concatenate([part for block in blocks for part in (block, core_swap(block))])


def chip_sum(chunk):
    rows = chunk.shape[0] // 2
    return chunk[:rows].astype(F32) + core_swap(chunk[rows:]).astype(F32)


def far_sums(chunk):
    parts = jnp.split(chunk, lax.axis_size("pair") - 1)
    return [chip_sum(part).astype(LOW) for part in parts]


def to_pairs(sums):
    count = lax.axis_size("pair")
    return [pair_from(part, count - shift) for shift, part in enumerate(sums, 1)]


def pipelined(block, work):
    arriving = from_pairs(block)
    near = on_chips([block])
    *near_out, last = work(near)
    arriving, last = pin(arriving, last)
    total = chip_sum(last)
    far = on_chips(arriving)
    *far_out, last = work(far)
    back = to_pairs(far_sums(last))
    return (near, far), (near_out, far_out), total, back


def arrived(total, back):
    return sum((part.astype(F32) for part in back), total)


def layer_norm(values, norm_gain, norm_shift):
    centered = values - jnp.mean(values, axis=-1, keepdims=True)
    inverse = lax.rsqrt(jnp.mean(centered * centered, axis=-1, keepdims=True) + EPS_NORM)
    normed = centered * inverse
    return (normed * norm_gain + norm_shift, normed, inverse)


def norm_backward(grad_out, normed, inverse, norm_gain):
    scaled = grad_out * norm_gain
    grad_in = inverse * (
        scaled
        - jnp.mean(scaled, axis=-1, keepdims=True)
        - normed * jnp.mean(scaled * normed, axis=-1, keepdims=True)
    )
    return (grad_in, jnp.sum(grad_out * normed, axis=0), jnp.sum(grad_out, axis=0))


def dot(left, right, dims):
    return lax.dot_general(left, right, (dims, ((), ())), preferred_element_type=F32)


def times(left, right):
    return dot(left, right, ((1,), (0,)))


def times_t(left, right):
    return dot(left, right, ((1,), (1,)))


def t_times(left, right):
    return dot(left, right, ((0,), (0,)))


LANES = 128
STEP = 352

def of_head(values, head):
    lane = lax.broadcasted_iota(jnp.int32, values.shape, 1)
    return jnp.where((lane < HD) == (head == 0), values, jnp.zeros_like(values))


def attend_kernel(q_ref, kn_ref, kf_ref, vn_ref, vf_ref, bn_ref, bf_ref, out_ref, lse_ref):
    query = q_ref[...]
    low_half = lax.broadcasted_iota(jnp.int32, (query.shape[0], LANES), 1) < HD
    tops, sums = [], []
    for head in range(2):
        one = of_head(query, head)
        scores = [
            times_t(one, k_ref[...]) + b_ref[...]
            for k_ref, b_ref in ((kn_ref, bn_ref), (kf_ref, bf_ref))
        ]
        top = jnp.maximum(*[jnp.max(s, axis=1, keepdims=True) for s in scores])
        total = jnp.zeros((query.shape[0], LANES), F32)
        for s, v_ref in zip(scores, (vn_ref, vf_ref)):
            value = v_ref[...]
            lane = lax.broadcasted_iota(jnp.int32, value.shape, 1)
            value = jnp.where((lane < HD) == (head == 0), value, jnp.ones_like(value))
            total = total + times(jnp.exp(s - top).astype(LOW), value)
        tops.append(top)
        sums.append(total)
    row_sum = pltpu.roll(jnp.where(low_half, sums[1], sums[0]), HD, 1)
    out_ref[...] = (jnp.where(low_half, sums[0], sums[1]) / row_sum).astype(LOW)
    lse_ref[...] = jnp.where(low_half, tops[0], tops[1]) + jnp.log(row_sum)


def attend(query, near, far, bias_near, bias_far):
    rows, width = query.shape[0], query.shape[1] // 3
    pairs = width // LANES

    def whole(array, offset):
        return pl.BlockSpec((array.shape[0], LANES), lambda p, i: (0, 3 * p + offset))

    def full(array):
        return pl.BlockSpec(array.shape, lambda p, i: (0, 0))

    block = pl.BlockSpec((min(STEP, rows), LANES), lambda p, i: (i, p))
    query_block = pl.BlockSpec(block.block_shape, lambda p, i: (i, 3 * p))
    return pl.pallas_call(
        attend_kernel,
        out_shape=(
            jax.ShapeDtypeStruct((rows, width), LOW),
            jax.ShapeDtypeStruct((rows, width), F32),
        ),
        grid=(pairs, pl.cdiv(rows, STEP)),
        in_specs=[
            query_block,
            whole(near, 1),
            whole(far, 1),
            whole(near, 2),
            whole(far, 2),
            full(bias_near),
            full(bias_far),
        ],
        out_specs=(block, block),
        compiler_params=pltpu.CompilerParams(vmem_limit_bytes=48 * 2**20),
        name="attend",
    )(query, near, far, near, far, bias_near, bias_far)


def attend_back_kernel(
    q_ref, k_ref, v_ref, bias_ref, do_ref, out_ref, lse_ref,
    grad_ref, sum_ref,
    lse_row, delta_row, dq_acc, sum_acc,
):
    step, steps = pl.program_id(1), pl.num_programs(1)
    block = k_ref.shape[0]
    query, grad = q_ref[...], do_ref[...]

    @pl.when(step == 0)
    def _():
        lse_row[...] = jnp.transpose(lse_ref[...])
        delta_row[...] = jnp.transpose(grad.astype(F32) * out_ref[...].astype(F32))
        dq_acc[...] = jnp.zeros_like(dq_acc)
        sum_acc[...] = jnp.zeros_like(sum_acc)

    key, value = k_ref[...], v_ref[...]
    key_turned = jnp.transpose(key.astype(F32)).astype(LOW)
    grad_key = jnp.zeros((block, LANES), F32)
    grad_value = jnp.zeros((block, LANES), F32)
    for head in range(2):
        lanes = pl.ds(head * HD, HD)
        query_one, grad_one = of_head(query, head), of_head(grad, head)
        soft = jnp.exp(times_t(key, query_one) + bias_ref[...] - lse_row[pl.ds(head * HD, 1), :])
        delta = jnp.sum(delta_row[lanes, :], axis=0, keepdims=True)
        slope = (soft * (times_t(value, grad_one) - delta)).astype(LOW)
        grad_value += times(soft.astype(LOW), grad_one)
        grad_key += times(slope, query_one)
        dq_acc[lanes, :] += times(key_turned[head * HD : (head + 1) * HD], slope)
    rows = pl.ds(pl.multiple_of(step * block, 16), block)
    grad_ref[rows, LANES : 2 * LANES] = grad_key.astype(LOW)
    grad_ref[rows, 2 * LANES :] = grad_value.astype(LOW)
    sum_acc[1:2, :] += jnp.sum(grad_value, axis=0, keepdims=True)

    @pl.when(step == steps - 1)
    def _():
        grad_query = jnp.transpose(dq_acc[...]) * HD**-0.5
        grad_ref[:, :LANES] = grad_query.astype(LOW)
        sum_acc[0:1, :] = jnp.sum(grad_query, axis=0, keepdims=True)
        sum_ref[...] = sum_acc[...]


def attend_back(projected, bias, grad_out, out, lse):
    rows, width = out.shape
    pairs, step = width // LANES, rows // 2

    def whole(scale):
        return pl.BlockSpec((rows, LANES), lambda p, i: (0, scale * p))

    def part(offset):
        return pl.BlockSpec((step, LANES), lambda p, i: (i, 3 * p + offset))

    return pl.pallas_call(
        attend_back_kernel,
        out_shape=(
            jax.ShapeDtypeStruct((rows, 3 * width), LOW),
            jax.ShapeDtypeStruct((8, width), F32),
        ),
        grid=(pairs, 2),
        in_specs=[
            whole(3),
            part(1),
            part(2),
            pl.BlockSpec((step, 1), lambda p, i: (i, 0)),
            whole(1),
            whole(1),
            whole(1),
        ],
        out_specs=(
            pl.BlockSpec((rows, 3 * LANES), lambda p, i: (0, p)),
            pl.BlockSpec((8, LANES), lambda p, i: (0, p)),
        ),
        scratch_shapes=[
            pltpu.VMEM((LANES, rows), F32),
            pltpu.VMEM((LANES, rows), F32),
            pltpu.VMEM((LANES, rows), F32),
            pltpu.VMEM((8, LANES), F32),
        ],
        compiler_params=pltpu.CompilerParams(vmem_limit_bytes=56 * 2**20),
        name="attend_back",
    )(projected, projected, projected, bias, grad_out, out, lse)


UNITS = 256


def gelu_and_slope(values):
    size = jnp.abs(values)
    below = 1.0 + (0.3275911 * 0.5**0.5) * size
    inner = pl.reciprocal(below, approx=True)
    inner = inner * (2.0 - below * inner)
    tail = 0.5 * 1.061405429
    for term in (-1.453152027, 1.421413741, -0.284496736, 0.254829592):
        tail = tail * inner + 0.5 * term
    bell = jnp.exp(-0.5 * values * values)
    tail = tail * inner * bell
    share = jnp.where(values < 0, tail, 1.0 - tail)
    return values * share, share + values * ((2 * math.pi) ** -0.5 * bell)


def hidden_kernel(rows_ref, own_up, own_down, far_up, far_down, bias_ref, low_ref, slope_ref, out_ref, total):
    step, steps = pl.program_id(0), pl.num_programs(0)

    @pl.when(step == 0)
    def _():
        total[...] = jnp.zeros_like(total)

    def work(up_ref, down_ref):
        value, slope = gelu_and_slope(times(rows_ref[...], up_ref[...]) + bias_ref[...])
        value = value.astype(LOW)
        low_ref[...] = value
        slope_ref[...] = slope.astype(LOW)
        total[...] += times_t(value, down_ref[...])

    @pl.when(step < steps // 2)
    def _():
        work(own_up, own_down)

    @pl.when(step >= steps // 2)
    def _():
        work(far_up, far_down)

    @pl.when(step == steps - 1)
    def _():
        out_ref[...] = total[...].astype(LOW)


def hidden_back_kernel(grad_ref, own_up, own_down, far_up, far_down, slope_ref, pre_ref, sum_ref, out_ref, total):
    step, steps = pl.program_id(0), pl.num_programs(0)

    @pl.when(step == 0)
    def _():
        total[...] = jnp.zeros_like(total)

    def work(up_ref, down_ref):
        grad_pre = times(grad_ref[...], down_ref[...]) * slope_ref[...].astype(F32)
        sum_ref[...] = jnp.broadcast_to(jnp.sum(grad_pre, axis=0, keepdims=True), sum_ref.shape)
        grad_pre = grad_pre.astype(LOW)
        pre_ref[...] = grad_pre
        total[...] += times_t(grad_pre, up_ref[...])

    @pl.when(step < steps // 2)
    def _():
        work(own_up, own_down)

    @pl.when(step >= steps // 2)
    def _():
        work(far_up, far_down)

    @pl.when(step == steps - 1)
    def _():
        out_ref[...] = total[...].astype(LOW)


def hidden_call(kernel, rows_in, sides, units, extra, extra_spec, outs, name):
    rows, width = rows_in.shape
    steps = units // UNITS
    half_steps = steps // 2
    block = pl.BlockSpec((rows, UNITS), lambda j: (0, j))
    whole = pl.BlockSpec((rows, width), lambda j: (0, 0))

    def part(at, begin):
        return pl.BlockSpec(
            (width, UNITS),
            lambda j: (0, at // UNITS + jnp.clip(j - begin, 0, half_steps - 1)),
        )

    specs, arrays = [], []
    for side, (array, at) in enumerate(sides):
        specs += [part(at, side * half_steps), part(at + units // 2, side * half_steps)]
        arrays += [array, array]
    return pl.pallas_call(
        kernel,
        out_shape=tuple(shape for shape, _ in outs),
        grid=(steps,),
        in_specs=[whole, *specs, extra_spec or block],
        out_specs=tuple(spec or block for _, spec in outs),
        scratch_shapes=[pltpu.VMEM((rows, width), F32)],
        compiler_params=pltpu.CompilerParams(vmem_limit_bytes=48 * 2**20),
        name=name,
    )(rows_in, *arrays, extra)


def hidden_layer(rows_in, sides, bias):
    rows, width = rows_in.shape
    units = jax.ShapeDtypeStruct((rows, bias.shape[1]), LOW)
    return hidden_call(
        hidden_kernel,
        rows_in,
        sides,
        bias.shape[1],
        bias,
        pl.BlockSpec((1, UNITS), lambda j: (0, j)),
        [
            (units, None),
            (units, None),
            (
                jax.ShapeDtypeStruct((rows, width), LOW),
                pl.BlockSpec((rows, width), lambda j: (0, 0)),
            ),
        ],
        "hidden_layer",
    )


def hidden_back(grad, sides, slope):
    rows, width = grad.shape
    grad_pre, total, out = hidden_call(
        hidden_back_kernel,
        grad,
        sides,
        slope.shape[1],
        slope,
        None,
        [
            (jax.ShapeDtypeStruct(slope.shape, LOW), None),
            (
                jax.ShapeDtypeStruct((8, slope.shape[1]), F32),
                pl.BlockSpec((8, UNITS), lambda j: (0, j)),
            ),
            (
                jax.ShapeDtypeStruct((rows, width), LOW),
                pl.BlockSpec((rows, width), lambda j: (0, 0)),
            ),
        ],
        "hidden_back",
    )
    return grad_pre, total[0], out


def gram_sum(partial, axes, aside):
    middle, quarter = partial.shape[0] // 2, partial.shape[0] // 4
    first_block, side_block = partial[:middle, :middle], partial[:middle, middle:]
    last_block = partial[middle:, middle:]
    if lax.axis_size("pair") != 2 or len(axes) > len(GROUP):
        return pin(lax.psum((first_block, side_block, last_block), axes), aside)
    first = lax.axis_index("core") == 0
    upper = jnp.concatenate([first_block, side_block[:quarter]])
    lower = jnp.concatenate([last_block, side_block[quarter:]])
    mine = jnp.where(first, upper, lower) + core_swap(jnp.where(first, lower, upper))
    far, aside = pin(pair_from(mine, 1), aside)
    mine = mine + far
    other = core_swap(mine)
    upper, lower = jnp.where(first, mine, other), jnp.where(first, other, mine)
    side_block = jnp.concatenate([upper[middle:], lower[middle:]])
    return (upper[:middle], side_block, lower[:middle]), aside


def sum_over(values, axes):
    for axis in axes:
        count, bit = lax.axis_size(axis), 1
        while bit < count:
            values = values + lax.ppermute(values, axis, [(i, i ^ bit) for i in range(count)])
            bit *= 2
    return values


def gram_of(matrix):
    low = matrix.astype(LOW)
    return times_t(low, low)


CHUNK = 256


def newton_schulz_kernel(
    first_ref, side_ref, last_ref, start_ref, out_ref,
    gram, poly, turn, gram_rest, poly_rest, turn_rest, current, current_low,
    gram_col, poly_col, turn_col, gram_row, poly_row,
):
    middle = first_ref.shape[0]
    chunks = 2 * middle // CHUNK
    gram[:middle, :middle] = first_ref[...]
    gram[:middle, middle:] = side_ref[...]
    gram[middle:, :middle] = jnp.transpose(side_ref[...])
    gram[middle:, middle:] = last_ref[...]
    on = lax.broadcasted_iota(jnp.int32, (CHUNK, CHUNK), 0) == lax.broadcasted_iota(
        jnp.int32, (CHUNK, CHUNK), 1
    )

    def part(i):
        return pl.ds(pl.multiple_of(i * CHUNK, CHUNK), CHUNK)

    def each(work):
        def step(i, carry):
            work(part(i))
            return carry

        lax.fori_loop(0, chunks, step, 0)

    def keep(rows, value, excess, whole, rest, col, row):
        whole[rows, :] = value
        rest[rows, :] = value.astype(LOW)
        block = whole[rows, rows] - jnp.where(on, excess, 0.0)
        whole[rows, rows] = block
        rest[rows, rows] = jnp.where(on, 0.0, block).astype(LOW)
        diagonal = jnp.where(on, block, 0.0)
        col[rows, :] = jnp.sum(diagonal, axis=1, keepdims=True)
        if row is not None:
            row[:, rows] = jnp.sum(diagonal, axis=0, keepdims=True)

    def product(rows, left, left_rest, left_col, right, right_rest, right_row):
        return (
            times(left_rest[rows, :], right_rest[...])
            + left_col[rows, :] * right[rows, :]
            + left[rows, :] * right_row[...]
        )

    trace = jnp.zeros((1, 1), F32)
    for i in range(chunks):
        at = slice(i * CHUNK, (i + 1) * CHUNK)
        diagonal = jnp.where(on, gram[at, at], 0.0)
        trace += jnp.sum(jnp.sum(diagonal, axis=1, keepdims=True), axis=0, keepdims=True)
    inverse = lax.rsqrt(trace + EPS_GRAM)

    def begin(rows):
        scaled = gram[rows, :] * (inverse * inverse)
        keep(rows, scaled, 0.0, gram, gram_rest, gram_col, gram_row)
        value = start_ref[rows, :] * inverse
        current[rows, :] = value
        current_low[0, rows, :] = value.astype(LOW)

    each(begin)

    def polynomial(rows):
        square = product(rows, gram, gram_rest, gram_col, gram, gram_rest, gram_row)
        excess = NS_C * gram_col[rows, :] * gram_col[rows, :]
        value = NS_B * gram[rows, :] + NS_C * square
        keep(rows, value, excess, poly, poly_rest, poly_col, poly_row)

    def advanced(rows, slot):
        moved = times(poly_rest[rows, :], current_low[slot])
        return (NS_A + poly_col[rows, :]) * current[rows, :] + moved

    def iterate(iteration, carry):
        slot = lax.rem(iteration, 2)
        each(polynomial)

        def advance(rows):
            value = advanced(rows, slot)
            current[rows, :] = value
            current_low[1 - slot, rows, :] = value.astype(LOW)

        each(advance)

        def first(rows):
            value = product(rows, poly, poly_rest, poly_col, gram, gram_rest, gram_row)
            excess = poly_col[rows, :] * gram_col[rows, :]
            keep(rows, NS_A * gram[rows, :] + value, excess, turn, turn_rest, turn_col, None)

        each(first)

        def second(rows):
            value = product(rows, turn, turn_rest, turn_col, poly, poly_rest, poly_row)
            excess = turn_col[rows, :] * poly_col[rows, :]
            keep(rows, NS_A * turn[rows, :] + value, excess, gram, gram_rest, gram_col, gram_row)

        each(second)
        return carry

    lax.fori_loop(0, NS_STEPS - 1, iterate, 0)
    each(polynomial)

    def finish(rows):
        out_ref[rows, :] = advanced(rows, (NS_STEPS - 1) % 2).astype(LOW)

    each(finish)


def orthogonalize(start, gram):
    size, width = start.shape
    square = [pltpu.VMEM((size, size), F32)] * 3 + [pltpu.VMEM((size, size), LOW)] * 3
    return pl.pallas_call(
        newton_schulz_kernel,
        out_shape=jax.ShapeDtypeStruct((size, width), LOW),
        in_specs=[pl.BlockSpec(memory_space=pltpu.VMEM)] * 4,
        out_specs=pl.BlockSpec(memory_space=pltpu.VMEM),
        scratch_shapes=square
        + [pltpu.VMEM((size, width), F32), pltpu.VMEM((2, size, width), LOW)]
        + [pltpu.VMEM((size, 1), F32)] * 3
        + [pltpu.VMEM((1, size), F32)] * 2,
        compiler_params=pltpu.CompilerParams(vmem_limit_bytes=56 * 2**20),
        name="newton_schulz",
    )(*gram, start)


def per_device(
    tokens,
    cotangent,
    attention_in,
    attention_out,
    hidden_up,
    hidden_down,
    attention_in_momentum,
    attention_out_momentum,
    hidden_up_momentum,
    hidden_down_momentum,
    row_params,
    column_bias,
    lengths,
):
    local_rows, image_count, _ = tokens.shape
    pair_count = lax.axis_size("pair")
    data_count = lax.axis_size("dp")
    half = lax.axis_index("half")
    layer_count = attention_in.shape[0]
    rows_owned = hidden_up.shape[1]
    head_own = column_bias.shape[1]
    heads = 2 * head_own
    head_width = heads * HD
    seq_total = local_rows * 4 * pair_count

    def away(values):
        own = jnp.where(half == 0, values[:, 0], values[:, 1])
        return own, jnp.where(half == 0, values[:, 1], values[:, 0]).astype(LOW)

    def together(own, other):
        return jnp.concatenate([own, other.astype(F32)], axis=0)

    def at_home(own, other):
        other = other.astype(F32)
        return jnp.where(
            half == 0, jnp.stack([own, other], axis=1), jnp.stack([other, own], axis=1)
        )

    place = []
    for shift in range(pair_count):
        chip = lax.rem(lax.axis_index("pair") + shift, pair_count)
        for flip in range(2):
            core = lax.axis_index("core") ^ flip
            for other in range(2):
                block = ((half ^ other) * pair_count + chip) * 2 + core
                place.append(block * local_rows + jnp.arange(local_rows, dtype=jnp.int32))
    length = jnp.where(half == 0, lengths[0], lengths[1])
    key_bias = jnp.where(jnp.concatenate(place) < length, 0.0, SCORE_FLOOR).astype(F32)
    near_rows = 4 * local_rows
    bias_near, bias_far = key_bias[None, :near_rows], key_bias[None, near_rows:]

    column_other = half_swap(column_bias)
    column_all = jnp.concatenate([column_bias, column_other], axis=1)
    data_index = lax.axis_index("dp")
    kinds = range(KINDS)
    side_width = 3 * head_own * HD
    by_side = head_own * HD == LANES
    matrix_count = layer_count * KINDS
    wide = data_count * 2 == matrix_count
    pad_width = hidden_up.shape[2]
    column_axes = GROUP if wide else GROUP + ("half",)

    def dp_xor(values, offset):
        return lax.ppermute(values, "dp", [(i, i ^ offset) for i in range(data_count)])

    def data_gather(piece):
        return lax.all_gather(piece, "dp", axis=0, tiled=True)

    def data_sum(partial):
        return lax.psum_scatter(partial, "dp", scatter_dimension=0, tiled=True)

    def sides(own, other):
        if not by_side:
            own, other = (w.reshape(-1, 3, head_own * HD) for w in (own, other))
        return jnp.concatenate([own, other], axis=-1).reshape(own.shape[0], 2 * side_width)

    def own_weights(block_index):
        first = attention_in[block_index].astype(LOW).reshape(rows_owned, head_own, 3, HD)
        first = jnp.swapaxes(first, 1, 2).reshape(rows_owned, -1)
        return (
            jnp.concatenate([first, attention_out[block_index].astype(LOW)], axis=1),
            jnp.concatenate(
                [hidden_up[block_index].astype(LOW), hidden_down[block_index].astype(LOW)], axis=1
            ),
        )

    def attention_matrices(own, other):
        return (
            sides(own[:, :side_width], other[:, :side_width]),
            jnp.concatenate([own[:, side_width:], other[:, side_width:]], axis=1),
        )

    moments_old = (
        attention_in_momentum,
        attention_out_momentum,
        hidden_up_momentum,
        hidden_down_momentum,
    )

    def padded(array):
        return jnp.pad(array, ((0, 0), (0, pad_width - array.shape[1])))

    def moment_away():
        first, second = (
            jnp.concatenate([m[layer] for m in moments_old], axis=1).astype(LOW)
            for layer in range(2)
        )
        return jnp.where(half == 0, first, second), jnp.where(half == 0, second, first)

    def moment_items(own, other):
        items, at = [], 0
        for kind, moment in enumerate(moments_old):
            width = moment.shape[2]
            if wide:
                pair = [padded(array[:, at : at + width]) for array in (own, other)]
                items.append((kind, jnp.concatenate(pair, axis=1)))
            else:
                items += [
                    (l * KINDS + kind, padded(moment[l].astype(LOW))) for l in range(layer_count)
                ]
            at += width
        return items

    def reordered(parts):
        bit = 1
        while bit < data_count:
            swap = (data_index & bit) != 0
            parts = [jnp.where(swap, parts[i ^ bit], part) for i, part in enumerate(parts)]
            bit *= 2
        return parts

    def to_owner(items):
        blocks = reordered([rows for _, rows in sorted(items, key=lambda item: item[0])])
        return [dp_xor(block, offset) if offset else block for offset, block in enumerate(blocks)]

    def from_owner(matrix):
        blocks = jnp.split(matrix, data_count)

        if not wide:
            parts = reordered([dp_xor(b, i) if i else b for i, b in enumerate(blocks)])
            return [parts[layer * KINDS : (layer + 1) * KINDS] for layer in range(layer_count)]
        far, near = [], []
        for offset, block in enumerate(blocks):
            pairs = [
                (2 * i + h, 2 * (i ^ offset) + 1 - h) for i in range(data_count) for h in range(2)
            ]
            far.append(lax.ppermute(block[:, pad_width:], ("dp", "half"), pairs))
        for offset, block in enumerate(blocks):
            near.append(
                dp_xor(block[:, :pad_width], offset) if offset else block[:, :pad_width]
            )
        near, far = reordered(near), reordered(far)
        return [
            [jnp.where(half == layer, n, f) for n, f in zip(near, far)]
            for layer in range(layer_count)
        ]

    own_low = [own_weights(block_index) for block_index in range(layer_count)]
    params = row_params
    part_of = jnp.arange(3 * head_width) % (3 * LANES) // LANES
    query_scale = jnp.where(part_of == 0, HD**-0.5, 1.0).astype(LOW)
    own_tokens, other_tokens = away(tokens)
    other_tokens = half_swap(other_tokens)
    first_own = data_gather(own_low[0][0])
    first_other = half_swap(own_low[0][0])
    first_own, first_other, own = pin(first_own, first_other, own_low[0][1])
    first_other = data_gather(first_other)
    hidden_other = half_swap(own)
    hidden_own = data_gather(own)
    residual = together(own_tokens, other_tokens)
    kept = []

    for block_index in range(layer_count):
        last = block_index == layer_count - 1
        row_set = params[block_index]
        col_set = column_all[block_index]
        unit_bias = col_set[:, 2 * HD :].reshape(1, -1)
        query_bias = col_set[:, :HD].reshape(-1, LANES)
        value_bias = col_set[:, HD : 2 * HD].reshape(-1, LANES)
        in_bias = jnp.concatenate(
            [query_bias, jnp.zeros_like(query_bias), value_bias], axis=1
        ).reshape(-1)
        norm_one, normed_first, inverse_first = layer_norm(residual, row_set[0], row_set[1])
        block = norm_one.astype(LOW)
        arriving = from_pairs(block)
        near = on_chips([block])
        w_in, w_out = attention_matrices(first_own, first_other)

        def project(rows):
            return (times(rows, w_in) + in_bias).astype(LOW) * query_scale

        query_near = project(near)
        if block_index > 0:
            query_near, own = pin(query_near, own_low[block_index][1])
            hidden_other = half_swap(own)
            hidden_own = data_gather(own)
        arriving, query_near = pin(arriving, query_near)
        far = on_chips(arriving)
        query_far = project(far)
        heads_far, lse_far = attend(query_far, query_near, query_far, bias_near, bias_far)
        if last:
            heads_far, hidden_other, (own_cotangent, other) = pin(
                heads_far, hidden_other, away(cotangent)
            )
            aside = half_swap(other)
        else:
            heads_far, hidden_other, first_own = pin(
                heads_far, hidden_other, own_low[block_index + 1][0]
            )
            aside = half_swap(first_own)
        hidden_other = data_gather(hidden_other)
        sums, query_held = pin(far_sums(times_t(heads_far, w_out).astype(LOW)), query_near)
        back = to_pairs(sums)
        heads_near, lse_near = attend(query_held, query_near, query_far, bias_near, bias_far)
        heads_near, back, aside = pin(heads_near, back, aside)
        if last:
            other_cotangent = aside
        else:
            first_own, first_other = jnp.split(
                data_gather(jnp.concatenate([first_own, aside], axis=1)), 2, axis=1
            )
        total = chip_sum(times_t(heads_near, w_out).astype(LOW))
        branch_one = arrived(total, back) + row_set[2]
        middle = residual + row_set[3] * branch_one
        norm_two, normed_second, inverse_second = layer_norm(middle, row_set[4], row_set[5])
        hidden_full = ((hidden_own, 0), (hidden_other, 0))
        second, second_out, total, back = pipelined(
            norm_two.astype(LOW),
            lambda rows: hidden_layer(rows, hidden_full, unit_bias),
        )
        branch_two = arrived(total, back) + row_set[6]
        residual = middle + row_set[7] * branch_two
        kept.append(
            (
                (w_in, w_out, hidden_full),
                normed_first,
                inverse_first,
                jnp.concatenate([near, far]),
                jnp.concatenate([query_near, query_far]),
                jnp.concatenate([lse_near, lse_far]),
                jnp.concatenate([heads_near, heads_far]),
                branch_one,
                normed_second,
                inverse_second,
                second,
                second_out,
                branch_two,
            )
        )
    grad_residual = together(own_cotangent, other_cotangent)

    row_terms = [None] * layer_count
    column_terms = [None] * layer_count
    owner_layers = [[None] * layer_count for _ in kinds]

    def to_half(reduced, layer):
        width = reduced.shape[1] // 2
        swapped = jnp.concatenate([reduced[:, width:], reduced[:, :width]], axis=1)
        return reduced, lax.ppermute(swapped, "half", [(1 - layer, layer)])

    def attention_grads(rows_in, rows_out, grad_proj, head_rows):
        in_grad, out_grad = t_times(rows_in, grad_proj), t_times(rows_out, head_rows)
        if not by_side:
            in_grad = in_grad.reshape(D, 3, 2, head_own * HD).transpose(0, 2, 1, 3).reshape(D, -1)
        first, second = jnp.split(in_grad, 2, axis=1), jnp.split(out_grad, 2, axis=1)
        return jnp.concatenate([first[0], second[0], first[1], second[1]], axis=1).astype(LOW)

    def settle(layer, both, part):
        full = both[0].astype(F32) + both[1].astype(F32)
        own, other = jnp.split(full, 2, axis=1)
        if part == "attention":
            owner_layers[0][layer] = (own[:, :side_width], other[:, :side_width])
            owner_layers[1][layer] = (own[:, side_width:], other[:, side_width:])
        else:
            owner_layers[part][layer] = (own, other)

    def heads_first(array):
        return jnp.swapaxes(array.reshape(-1, 3, head_own, HD), 1, 2).reshape(array.shape)

    def give_back(layer, owned):
        sent = jnp.concatenate([owned[k][layer][1].astype(LOW) for k in kinds], axis=1)
        return lax.ppermute(sent, "half", [(layer, 1 - layer)])

    def home_grads(layer, arrived_low):
        grads, at = [], 0
        for kind in kinds:
            own = owner_layers[kind][layer][0]
            width = own.shape[1]
            own = jnp.where(half == layer, own, arrived_low[:, at : at + width].astype(F32))
            at += width
            grads.append(heads_first(own) if kind == 0 else own)
        return grads

    def owner_items(kind):
        pair = [
            jnp.where(half == 0, first, second).astype(LOW)
            for first, second in zip(*owner_layers[kind])
        ]
        if kind == 0:
            pair = [heads_first(part) for part in pair]
        return [(kind, jnp.concatenate([padded(part) for part in pair], axis=1))]

    top = layer_count - 1
    for block_index in reversed(range(layer_count)):
        last = block_index == top
        (
            (w_in, w_out, hidden_full),
            normed_first,
            inverse_first,
            first,
            projected,
            lse,
            head_rows,
            branch_one,
            normed_second,
            inverse_second,
            second,
            second_out,
            branch_two,
        ) = kept[block_index]
        row_set = params[block_index]
        near_rows = 4 * local_rows
        grad_two = grad_residual * row_set[7]
        slopes = iter([chunk[1] for chunk in second_out])
        reach, back_out, total, back = pipelined(
            grad_two.astype(LOW),
            lambda rows: hidden_back(rows, hidden_full, next(slopes)),
        )
        scale_two = jnp.sum(grad_residual * branch_two, axis=0)
        shift_down = jnp.sum(grad_two, axis=0)
        unit_grad = sum(chunk[1] for chunk in back_out)
        down_grad = t_times(jnp.concatenate(reach), jnp.concatenate([c[0] for c in second_out]))
        back, down_grad = pin(back, down_grad.astype(LOW))
        if not last:
            down_sum = data_sum(down_grad)
            back, sums_late = pin(back, jnp.split(sums_late, 3))
            down_late = to_half(sums_late[0], top)
        grad_norm = arrived(total, back)
        grad_in, gain_two, shift_two = norm_backward(
            grad_norm, normed_second, inverse_second, row_set[4]
        )
        grad_residual = grad_residual + grad_in

        grad_one = grad_residual * row_set[3]
        block = grad_one.astype(LOW)
        arriving = from_pairs(block)
        scale_one = jnp.sum(grad_residual * branch_one, axis=0)
        shift_out = jnp.sum(grad_one, axis=0)
        near = on_chips([block])
        heads_near = times(near, w_out).astype(LOW)
        up_grad = t_times(jnp.concatenate(second), jnp.concatenate([c[0] for c in back_out]))
        arriving, heads_near, up_grad = pin(arriving, heads_near, up_grad.astype(LOW))
        if not last:
            heads_near, down_late = pin(heads_near, down_late)
            settle(top, down_late, 3)
            up_late = to_half(sums_late[1], top)
        far = on_chips(arriving)
        grad_heads = jnp.concatenate([heads_near, times(far, w_out).astype(LOW)])
        if not last:
            up_sum = data_sum(up_grad)
            grad_heads, down_sum = pin(grad_heads, down_sum)
            down_half = to_half(down_sum, block_index)
        if last:
            grad_heads, (own_moment, away_moment) = pin(grad_heads, moment_away())
            other_moment = half_swap(away_moment)
        else:
            grad_heads, own_moment, other_moment = pin(grad_heads, own_moment, other_moment)
            owner_moment = to_owner(moment_items(own_moment, other_moment))
        grad_proj, head_sums = attend_back(projected, key_bias[:, None], grad_heads, head_rows, lse)
        if last:
            grad_proj, other_moment, residual = pin(grad_proj, other_moment, residual)
            output_other = half_swap(residual[local_rows:].astype(LOW))
        else:
            grad_proj, owner_moment, up_late, down_half, up_sum = pin(
                grad_proj, owner_moment, up_late, down_half, up_sum
            )
            up_half = to_half(up_sum, block_index)
            settle(top, up_late, 2)
            attention_late = to_half(sums_late[2], top)
        reach = jnp.concatenate([near, far])
        if not last:
            attention_low = attention_grads(first, reach, grad_proj, head_rows)
            attention_low, grad_proj = pin(attention_low, grad_proj)
            attention_sum = data_sum(attention_low)
        sums, (grad_proj, reach, head_rows, first) = pin(
            far_sums(times_t(grad_proj[near_rows:], w_in).astype(LOW)),
            (grad_proj, reach, head_rows, first),
        )
        back = to_pairs(sums)
        total = chip_sum(times_t(grad_proj[:near_rows], w_in).astype(LOW))
        if last:
            attention_low = attention_grads(first, reach, grad_proj, head_rows)
            blocks = zip(*[jnp.split(g, data_count) for g in (down_grad, up_grad, attention_low)])
            sums_late = data_sum(jnp.concatenate([g for block in blocks for g in block]))
            back, total, attention_low, output_other = pin(back, total, attention_low, output_other)
            layer_output = at_home(residual[:local_rows], output_other)
        else:
            settle(block_index, down_half, 3)
            total, attention_late, up_half = pin(total, attention_late, up_half)
            settle(top, attention_late, "attention")
            settle(block_index, up_half, 2)
            total, attention_sum = pin(total, attention_sum)
            attention_half = to_half(attention_sum, 0)
            back, total = pin(back, total)
        grad_norm = sum((part.astype(F32) for part in back), total)
        grad_in, gain_one, shift_one = norm_backward(
            grad_norm, normed_first, inverse_first, row_set[0]
        )
        grad_residual = grad_residual + grad_in
        row_terms[block_index] = jnp.stack(
            [
                gain_one,
                shift_one,
                shift_out,
                scale_one,
                gain_two,
                shift_two,
                shift_down,
                scale_two,
            ]
        )
        column_terms[block_index] = jnp.concatenate(
            [
                head_sums[0].reshape(heads, HD),
                head_sums[1].reshape(heads, HD),
                unit_grad.reshape(heads, -1),
            ],
            axis=1,
        )
    settle(0, attention_half, "attention")
    if wide:
        owner_grad = to_owner([item for kind in kinds for item in owner_items(kind)])
        owner_grad, owner_layers, grad_residual, row_terms, column_terms = pin(
            owner_grad, owner_layers, grad_residual, row_terms, column_terms
        )
    else:
        grads = [home_grads(layer, give_back(layer, owner_layers)) for layer in range(layer_count)]
        owner_grad = to_owner(
            [
                (layer * KINDS + kind, padded(grads[layer][kind].astype(LOW)))
                for layer in range(layer_count)
                for kind in kinds
            ]
        )
    start = jnp.concatenate(
        [MOMENTUM * m.astype(F32) + g.astype(F32) for m, g in zip(owner_moment, owner_grad)]
    )
    gram_part = gram_of(start)
    grad_residual, row_terms, column_terms, gram_part = pin(
        grad_residual, row_terms, column_terms, gram_part
    )
    columns = jnp.stack(column_terms)
    flat = jnp.pad(columns.reshape(-1), (0, -columns.size % D)).reshape(-1, D)
    small = sum_over(jnp.concatenate([jnp.stack(row_terms).reshape(-1, D), flat]), ("dp",))
    rows_small = 8 * layer_count
    columns = small[rows_small:].reshape(-1)[: columns.size].reshape(columns.shape)
    owned_width = column_bias.shape[2] // data_count
    columns = lax.dynamic_slice_in_dim(columns, data_index * owned_width, owned_width, 2)
    column_grad = columns[:, :head_own] + half_swap(columns[:, head_own:])
    row_grad = sum_over(small[:rows_small], ("core", "pair", "half")).reshape(row_params.shape)
    gram, (row_grad, column_grad) = gram_sum(gram_part, column_axes, (row_grad, column_grad))
    tokens_other = grad_residual[local_rows:].astype(LOW)
    gram, row_grad, column_grad, tokens_other, owner_layers = pin(
        gram, row_grad, column_grad, tokens_other, owner_layers
    )
    tokens_other = half_swap(tokens_other)
    returning = [give_back(layer, owner_layers) for layer in range(layer_count)] if wide else []
    finish, returning, tokens_other = pin(orthogonalize(start, gram), returning, tokens_other)
    returned = from_owner(finish)
    if wide:
        grads = [home_grads(layer, arrived_low) for layer, arrived_low in enumerate(returning)]
    tokens_grad = at_home(grad_residual[:local_rows], tokens_other)
    grads = [jnp.stack(layers) for layers in zip(*grads)]
    moments = [MOMENTUM * m + g for m, g in zip(moments_old, grads)]
    olds = (attention_in, attention_out, hidden_up, hidden_down)
    fans = (D, D // 16, D, FF)
    news = []
    for kind in range(KINDS):
        width = olds[kind].shape[2]
        rate = MUON_RATE * math.sqrt(max(D, width * 4 * pair_count) / fans[kind])
        step = jnp.stack([returned[layer][kind][:, :width] for layer in range(layer_count)])
        news.append(olds[kind] - rate * step.astype(F32))
    small_rate = 0.3 / math.sqrt(image_count * data_count * seq_total)
    row_new = row_params - small_rate * row_grad
    owned_width = column_grad.shape[2]
    column_old = lax.dynamic_slice_in_dim(
        column_bias, lax.axis_index("dp") * owned_width, owned_width, 2
    )
    column_new = column_old - small_rate * column_grad
    return (
        layer_output,
        tokens_grad,
        *grads,
        *moments,
        *news,
        row_grad,
        row_new,
        column_grad,
        column_new,
    )


def solution(mesh):
    data_count, tensor_count = mesh.shape["dp"], mesh.shape["tensor"]
    cut = Mesh(mesh.devices.reshape(data_count, 2, tensor_count // 4, 2), ALL)
    tensor = ("half", "pair", "core")
    token_spec = P(tensor, "dp", None)
    matrix_spec = P(None, "dp", tensor)
    in_specs = (
        (token_spec,) * 2 + (matrix_spec,) * 8 + (P(), P(None, tensor, None), P("dp"))
    )
    out_specs = (
        (token_spec,) * 2 + (matrix_spec,) * 12 + (P(), P()) + (P(None, tensor, "dp"),) * 2
    )
    return jax.shard_map(
        per_device, mesh=cut, in_specs=in_specs, out_specs=out_specs, check_vma=False
    )
```
